32 devices in a mesh: video: 2 (over x), frame: 4 (over z), head: 4 (over y, core).
Axes of the slice: x: 2, y: 2, z: 4, core: 2. Of those that a mesh axis runs over, the one named last changes fastest.
Arguments:
- query: bfloat16 [12288, 3072], P(('video', 'frame'), 'head'), parts along dimension 0, may hold values from -100 to 100
- keys: bfloat16 [12288, 3072], P(('video', 'frame'), 'head'), parts along dimension 0, may hold values from -4.04 to 4.04
- values: bfloat16 [12288, 3072], P(('video', 'frame'), 'head'), parts along dimension 0, may hold values from -6 to 6
- out_weight: bfloat16 [3072, 3072], P('head'), may hold values from -0.5 to 0.5
- tile_lists: int32 [32, 8], P(('video', 'frame')), parts along dimension 0, may hold values from 0 to 15, as said below
Outputs:
- mixed: bfloat16 [12288, 3072], P(('video', 'frame', 'head')), parts along dimension 0
The draws below stay inside these ranges and needn't reach their ends.
There are 2 independent parts, one for each index of `video`. The reference program is written for one: setup_inputs(seed, part) draws one part's arguments, and reference() takes and returns one part's arrays. A program takes and returns all parts, laid end to end along the dimension named above; an argument that names none is the same for every part. Nothing has to cross between parts.
Inputs may be any that keep to these rules, and one draw needn't show every extreme that they name: `tile_lists`: row t names 8 different tiles; the first is tile t itself, the second lies exactly 1 slabs from tile t's slab, and all lie at most 1 slabs from it (the slab of tile u is u // 4).
All inputs are finite; a program needn't handle non-finite values.
Results may differ from the reference program's by a relative error of at most 0.017.
Values may be sent and summed in bfloat16 or wider, within the bound.
A program may use at most 192 MiB of HBM per device.

```python
import math
import jax
import jax.numpy as jnp
from jax import lax

D = 3072
HEADS = 24
HD = 128
TPS = 4
TILE = 384
REACH = 1
KT = 8
NTILES = 16
TOKENS = 6144
HEAD_COLS = 768


def shared_base(key):
    return jnp.clip(jax.random.normal(key, (TOKENS, HEADS * HD), jnp.float32), -4.0, 4.0)


def draw_keys(key, part):
    base = shared_base(key)
    return base.astype(jnp.bfloat16)


def draw_query(key, part):
    key = jax.random.fold_in(key, 7)
    first_key = jax.random.fold_in(key, 0)
    result = 2.0 * jnp.clip(jax.random.normal(first_key, (TOKENS, HEADS * HD), jnp.float32), -4.0, 4.0)
    return result.astype(jnp.bfloat16)


def draw_tile_lists(key, part):
    key = jax.random.fold_in(key, 5)
    spot_key, noise_key = jax.random.split(key)
    slab_count = NTILES // TPS
    tile_ids = jnp.arange(NTILES, dtype=jnp.int32)
    tile_slab = tile_ids // TPS
    candidate = jnp.arange((2 * REACH + 1) * TPS, dtype=jnp.int32)
    target = tile_slab[:, None] + candidate[None, :] // TPS - REACH
    usable = (target >= 0) & (target < slab_count)
    far_offset = jnp.where(tile_slab + REACH < slab_count, REACH, -REACH)
    far_spot = jax.random.randint(spot_key, (NTILES,), 0, TPS, dtype=jnp.int32)
    far_cand = (far_offset + REACH) * TPS + far_spot
    own_cand = REACH * TPS + tile_ids % TPS
    noise = jax.random.randint(noise_key, (NTILES, (2 * REACH + 1) * TPS), 0, 1 << 19, dtype=jnp.int32)
    ranking = noise * 1024 + candidate[None, :]
    ranking = jnp.where(usable, ranking, (1 << 30) + candidate[None, :])
    ranking = jnp.where(candidate[None, :] == far_cand[:, None], -1, ranking)
    ranking = jnp.where(candidate[None, :] == own_cand[:, None], -2, ranking)
    picked = jnp.argsort(ranking, axis=1, stable=True)[:, :KT].astype(jnp.int32)
    chosen = (tile_slab[:, None] + picked // TPS - REACH) * TPS + picked % TPS
    return chosen.astype(jnp.int32)


def levels(own_key, shape, shards, smallest, top_value):
    def one(dim, shards_of):
        draws = jax.random.uniform(jax.random.fold_in(jax.random.fold_in(own_key, 6), dim), (shards_of,), jnp.float32, smallest / len(shards), top_value / len(shards))
        return jnp.repeat(jnp.exp(draws), shape[dim] // shards_of).reshape((-1,) + (1,) * (len(shape) - dim - 1))

    loudness = one(*shards[0])
    for cut in shards[1:]:
        loudness = loudness * one(*cut)
    return loudness


def gaussian(key, shape, deviation, bound, pieces=(), kind=jnp.bfloat16):
    loudness = levels(key, shape, pieces, -0.22, 0.18) if pieces else 1.0
    values = jax.random.normal(key, shape, jnp.float32) * deviation * loudness
    return jnp.minimum(jnp.maximum(values, -bound), bound).astype(kind)


def setup_inputs(seed: int = 0, part: int = 0) -> dict:
    seeds = jax.random.split(jax.random.key(seed), 6)
    part_keys = jax.random.split(jax.random.fold_in(seeds[5], part), 6)
    return {
        "query": draw_query(jax.random.fold_in(jax.random.fold_in(seeds[5], part), 71), part),
        "keys": draw_keys(jax.random.fold_in(jax.random.fold_in(seeds[5], part), 71), part),
        "values": gaussian(part_keys[2], (TOKENS, HEADS * HD), 1.0, 6.0, ((0, 4), (1, 4))),
        "out_weight": gaussian(seeds[3], (HEADS * HD, D), HD ** -0.5, 0.5, ((0, 4),)),
        "tile_lists": draw_tile_lists(jax.random.fold_in(jax.random.fold_in(seeds[5], part), 71), part),
    }


def reference(query, keys, values, out_weight, tile_lists):
    score_scale = 1.0 / math.sqrt(HD)
    query_tiles = query.reshape(NTILES, TILE, HEADS, HD)
    key_tiles = keys.reshape(NTILES, TILE, HEADS, HD)
    value_tiles = values.reshape(NTILES, TILE, HEADS, HD)

    def one_tile(block):
        query_tile, id_row = block
        key_rows = key_tiles[id_row].reshape(KT * TILE, HEADS, HD).astype(jnp.float32)
        value_rows = value_tiles[id_row].reshape(KT * TILE, HEADS, HD).astype(jnp.float32)
        scores = jnp.einsum('qhd,khd->hqk', query_tile.astype(jnp.float32), key_rows) * score_scale
        row_max = lax.optimization_barrier(jnp.max(scores, axis=-1, keepdims=True))
        exp_scores = jnp.exp(scores - row_max)
        row_total = lax.optimization_barrier(jnp.sum(exp_scores, axis=-1, keepdims=True))
        weights = lax.optimization_barrier(exp_scores.astype(jnp.bfloat16)).astype(jnp.float32)
        mixed_tile = jnp.einsum('hqk,khd->qhd', weights, value_rows) / jnp.transpose(row_total, (1, 0, 2))
        return mixed_tile.astype(jnp.bfloat16)
    attended = lax.map(one_tile, (query_tiles, tile_lists)).reshape(TOKENS, HEADS * HD)
    running_sum = jnp.zeros((TOKENS, D), jnp.float32)
    for group_index in range(HEADS * HD // HEAD_COLS):
        first_col = group_index * HEAD_COLS
        partial_sum = jnp.dot(attended[:, first_col:first_col + HEAD_COLS], out_weight[first_col:first_col + HEAD_COLS], preferred_element_type=jnp.float32)
        running_sum = running_sum + lax.optimization_barrier(partial_sum.astype(jnp.bfloat16)).astype(jnp.float32)
    return running_sum.astype(jnp.bfloat16)
```

```python
import functools
import math

import jax
import jax.numpy as jnp
from jax import lax
from jax.experimental import pallas as pl
from jax.experimental.pallas import tpu as pltpu
from jax.sharding import PartitionSpec as P

HD = 128
TILE = 384
MESH = pl.DeviceIdType.MESH
EXP2_SCALE = math.log2(math.e) / math.sqrt(HD)


def attention_kernel(
    frames, groups, reach, ids_ref, q_ref, k_hbm, v_hbm, out_ref,
    kbank, vbank, kcur, vcur, att, s0, s1,
    kv_send, kv_recv, own_sem, a_send, a_recv, a_own,
):
    tokens, cols = q_ref.shape
    heads = cols // HD
    tiles = tokens // TILE
    listed = ids_ref.shape[1]
    rows_out = tokens // groups
    owners_per_tile = TILE // rows_out
    slab = lax.axis_index("frame")
    group = lax.axis_index("head")
    offsets = [d for r in range(1, reach + 1) for d in (-r, r)]
    stores = ((k_hbm, kbank), (v_hbm, vbank))

    def exists(d):
        return (slab + d >= 0) & (slab + d < frames)

    def lanes(h):
        return pl.ds(pl.multiple_of(h * HD, HD), HD)

    def send_kv(h, d, kv):
        src, bank = stores[kv]
        return pltpu.make_async_remote_copy(
            src_ref=src.at[:, lanes(h)],
            dst_ref=bank.at[h, pl.ds((reach - d) * tokens, tokens), :],
            send_sem=kv_send.at[h, reach + d, kv],
            recv_sem=kv_recv.at[h, reach - d, kv],
            device_id={"frame": slab + d},
            device_id_type=MESH,
        )

    def recv_kv(h, d, kv):
        src, bank = stores[kv]
        return pltpu.make_async_remote_copy(
            src_ref=src.at[:, lanes(h)],
            dst_ref=bank.at[h, pl.ds((reach + d) * tokens, tokens), :],
            send_sem=kv_send.at[h, reach + d, kv],
            recv_sem=kv_recv.at[h, reach + d, kv],
            device_id={"frame": slab + d},
            device_id_type=MESH,
        )

    def own_kv(h, kv):
        src, bank = stores[kv]
        return pltpu.make_async_copy(
            src.at[:, lanes(h)],
            bank.at[h, pl.ds(reach * tokens, tokens), :],
            own_sem.at[h, kv],
        )

    def send_att(h, owner):
        return pltpu.make_async_remote_copy(
            src_ref=att.at[h, pl.ds(owner * rows_out, rows_out), :],
            dst_ref=out_ref.at[:, lanes(group * heads + h)],
            send_sem=a_send.at[h, owner],
            recv_sem=a_recv.at[h, group],
            device_id={"head": owner},
            device_id_type=MESH,
        )

    def recv_att(h, sender):
        return pltpu.make_async_remote_copy(
            src_ref=att.at[h, pl.ds(0, rows_out), :],
            dst_ref=out_ref.at[:, lanes(sender * heads + h)],
            send_sem=a_send.at[h, sender],
            recv_sem=a_recv.at[h, sender],
            device_id={"head": sender},
            device_id_type=MESH,
        )

    def own_att(h, owner):
        return pltpu.make_async_copy(
            att.at[h, pl.ds(owner * rows_out, rows_out), :],
            out_ref.at[:, lanes(owner * heads + h)],
            a_own.at[h],
        )

    def issue(h):
        for kv in range(2):
            for d in offsets:
                @pl.when(exists(d))
                def _(d=d, kv=kv):
                    send_kv(h, d, kv).start()
            own_kv(h, kv).start()

    barrier = pltpu.get_barrier_semaphore()
    for d in offsets:
        @pl.when(exists(d))
        def _(d=d):
            pl.semaphore_signal(barrier, inc=1, device_id={"frame": slab + d}, device_id_type=MESH)
    for g in range(groups):
        @pl.when(group != g)
        def _(g=g):
            pl.semaphore_signal(barrier, inc=1, device_id={"head": g}, device_id_type=MESH)
    below = jnp.minimum(slab, reach)
    above = jnp.minimum(frames - 1 - slab, reach)
    pl.semaphore_wait(barrier, groups - 1 + below + above)

    issue(0)
    if heads > 1:
        issue(1)
    vcur[:, :, HD:] = jnp.ones((vcur.shape[0], TILE, HD), vcur.dtype)

    def one_head(h, carry):
        for kv in range(2):
            own_kv(h, kv).wait()
            for d in offsets:
                @pl.when(exists(d))
                def _(d=d, kv=kv):
                    recv_kv(h, d, kv).wait_recv()
        for kv in range(2):
            for d in offsets:
                @pl.when(exists(d))
                def _(d=d, kv=kv):
                    send_kv(h, d, kv).wait_send()

        @pl.when(h + 2 < heads)
        def _():
            issue(h + 2)

        for d in [0] + offsets:
            @pl.when(exists(d))
            def _(d=d):
                for tile in range((reach + d) * tiles, (reach + d + 1) * tiles):
                    rows = slice(tile * TILE, (tile + 1) * TILE)
                    kcur[tile] = kbank[h, rows, :]
                    vcur[tile, :, :HD] = vbank[h, rows, :]

        scratch = (s0, s1)

        def score(t, j, tops):
            s_ref = scratch[t % 2]
            q_tile = q_ref[t * TILE:(t + 1) * TILE, lanes(h)]
            s = lax.dot_general(
                q_tile, kcur[ids_ref[t, j]],
                (((1,), (1,)), ((), ())), preferred_element_type=jnp.float32,
            )
            s_ref[:, j * TILE:(j + 1) * TILE] = s
            for c in range(TILE // HD):
                part = s[:, c * HD:(c + 1) * HD]
                tops = part if tops is None else jnp.maximum(tops, part)
            return tops

        tops = None
        for j in range(listed):
            tops = score(0, j, tops)
        for t in range(tiles):
            row_max = jnp.max(tops, axis=1, keepdims=True)
            tops = None
            total = None
            for j in range(listed):
                if t + 1 < tiles:
                    tops = score(t + 1, j, tops)
                s = scratch[t % 2][:, j * TILE:(j + 1) * TILE]
                weights = jnp.exp2((s - row_max) * EXP2_SCALE).astype(jnp.bfloat16)
                term = jnp.dot(weights, vcur[ids_ref[t, j]], preferred_element_type=jnp.float32)
                total = term if total is None else total + term
            att[h, t * TILE:(t + 1) * TILE, :] = (total[:, :HD] / total[:, HD:]).astype(att.dtype)
            for owner in range(t * owners_per_tile, (t + 1) * owners_per_tile):
                @pl.when(group != owner)
                def _(owner=owner):
                    send_att(h, owner).start()

                @pl.when(group == owner)
                def _(owner=owner):
                    own_att(h, owner).start()
        return carry

    lax.fori_loop(0, heads, one_head, 0)

    def finish(h, carry):
        for g in range(groups):
            @pl.when(group != g)
            def _(g=g):
                recv_att(h, g).wait_recv()
                send_att(h, g).wait_send()

            @pl.when(group == g)
            def _(g=g):
                own_att(h, g).wait()
        return carry

    lax.fori_loop(0, heads, finish, 0)


def on_device(query, keys, values, out_weight, tile_lists):
    frames = lax.axis_size("frame")
    groups = lax.axis_size("head")
    my_slab = lax.axis_index("frame")
    reach = min(2, (frames - 2) // 2)
    tokens, cols = query.shape
    heads = cols // HD
    tiles = tokens // TILE
    listed = tile_lists.shape[1]
    rows_out = tokens // groups
    bank_rows = (2 * reach + 1) * tokens
    full_weight = lax.all_gather(out_weight, "head", axis=0, tiled=True)
    ids = (tile_lists // tiles - my_slab + reach) * tiles + tile_lists % tiles
    attended = pl.pallas_call(
        functools.partial(attention_kernel, frames, groups, reach),
        out_shape=jax.ShapeDtypeStruct((rows_out, cols * groups), jnp.bfloat16),
        in_specs=[
            pl.BlockSpec(memory_space=pltpu.SMEM),
            pl.BlockSpec(memory_space=pltpu.VMEM),
            pl.BlockSpec(memory_space=pl.ANY),
            pl.BlockSpec(memory_space=pl.ANY),
        ],
        out_specs=pl.BlockSpec(memory_space=pl.ANY),
        scratch_shapes=[
            pltpu.VMEM((heads, bank_rows, HD), jnp.bfloat16),
            pltpu.VMEM((heads, bank_rows, HD), jnp.bfloat16),
            pltpu.VMEM((bank_rows // TILE, TILE, HD), jnp.bfloat16),
            pltpu.VMEM((bank_rows // TILE, TILE, 2 * HD), jnp.bfloat16),
            pltpu.VMEM((heads, tokens, HD), jnp.bfloat16),
            pltpu.VMEM((TILE, listed * TILE), jnp.float32),
            pltpu.VMEM((TILE, listed * TILE), jnp.float32),
            pltpu.SemaphoreType.DMA((heads, 2 * reach + 1, 2)),
            pltpu.SemaphoreType.DMA((heads, 2 * reach + 1, 2)),
            pltpu.SemaphoreType.DMA((heads, 2)),
            pltpu.SemaphoreType.DMA((heads, groups)),
            pltpu.SemaphoreType.DMA((heads, groups)),
            pltpu.SemaphoreType.DMA((heads,)),
        ],
        compiler_params=pltpu.CompilerParams(
            collective_id=0, has_side_effects=True, vmem_limit_bytes=56 * 1024 * 1024
        ),
        cost_estimate=pl.CostEstimate(
            flops=4 * tokens * listed * TILE * cols,
            bytes_accessed=8 * tokens * cols,
            transcendentals=tokens * listed * TILE * heads,
        ),
    )(ids, query, keys, values)
    return jnp.dot(attended, full_weight, preferred_element_type=jnp.float32).astype(jnp.bfloat16)


def solution(mesh):
    return jax.shard_map(
        on_device,
        mesh=mesh,
        in_specs=(
            P(("video", "frame"), "head"),
            P(("video", "frame"), "head"),
            P(("video", "frame"), "head"),
            P("head", None),
            P(("video", "frame"), None),
        ),
        out_specs=P(("video", "frame", "head"), None),
        check_vma=False,
    )
```

```python
import functools
import math

import jax
import jax.numpy as jnp
from jax import lax
from jax.experimental import pallas as pl
from jax.experimental.pallas import tpu as pltpu
from jax.sharding import PartitionSpec as P

HD = 128
TILE = 384
MESH = pl.DeviceIdType.MESH
EXP2_SCALE = math.log2(math.e) / math.sqrt(HD)


def attention_kernel(
    frames, groups, videos, reach, ids_ref, q_ref, k_hbm, v_hbm, w_hbm, out_ref,
    kbank, vbank, kcur, vcur, att, s0, s1, abank, wbank, acc,
    kv_send, kv_recv, own_sem, a_send, a_recv, a_own,
    w_own, pair_send, pair_recv, row_send, row_recv, spread_send, spread_recv, last_send, last_recv,
):
    tokens, cols = q_ref.shape
    heads = cols // HD
    tiles = tokens // TILE
    listed = ids_ref.shape[1]
    rows_out = tokens // groups
    owners_per_tile = TILE // rows_out
    slab = lax.axis_index("frame")
    group = lax.axis_index("head")
    video = lax.axis_index("video")
    core = group % 2
    row = group // 2
    rows_of_chips = groups // 2
    sibling = row * 2 + 1 - core
    part_rows = HD // videos
    width = acc.shape[1]
    offsets = [d for r in range(1, reach + 1) for d in (-r, r)]
    stores = ((k_hbm, kbank), (v_hbm, vbank))

    def exists(d):
        return (slab + d >= 0) & (slab + d < frames)

    def lanes(h):
        return pl.ds(pl.multiple_of(h * HD, HD), HD)

    def send_kv(h, d, kv):
        src, bank = stores[kv]
        return pltpu.make_async_remote_copy(
            src_ref=src.at[:, lanes(h)],
            dst_ref=bank.at[h, pl.ds((reach - d) * tokens, tokens), :],
            send_sem=kv_send.at[h, reach + d, kv],
            recv_sem=kv_recv.at[h, reach - d, kv],
            device_id={"frame": slab + d},
            device_id_type=MESH,
        )

    def recv_kv(h, d, kv):
        src, bank = stores[kv]
        return pltpu.make_async_remote_copy(
            src_ref=src.at[:, lanes(h)],
            dst_ref=bank.at[h, pl.ds((reach + d) * tokens, tokens), :],
            send_sem=kv_send.at[h, reach + d, kv],
            recv_sem=kv_recv.at[h, reach + d, kv],
            device_id={"frame": slab + d},
            device_id_type=MESH,
        )

    def own_kv(h, kv):
        src, bank = stores[kv]
        return pltpu.make_async_copy(
            src.at[:, lanes(h)],
            bank.at[h, pl.ds(reach * tokens, tokens), :],
            own_sem.at[h, kv],
        )

    def send_att(h, owner):
        return pltpu.make_async_remote_copy(
            src_ref=att.at[h, pl.ds(owner * rows_out, rows_out), :],
            dst_ref=abank.at[h, :, lanes(group)],
            send_sem=a_send.at[h, owner],
            recv_sem=a_recv.at[h, group],
            device_id={"head": owner},
            device_id_type=MESH,
        )

    def recv_att(h, sender):
        return pltpu.make_async_remote_copy(
            src_ref=att.at[h, pl.ds(0, rows_out), :],
            dst_ref=abank.at[h, :, lanes(sender)],
            send_sem=a_send.at[h, sender],
            recv_sem=a_recv.at[h, sender],
            device_id={"head": sender},
            device_id_type=MESH,
        )

    def own_att(h, owner):
        return pltpu.make_async_copy(
            att.at[h, pl.ds(owner * rows_out, rows_out), :],
            abank.at[h, :, lanes(owner)],
            a_own.at[h],
        )

    def issue(h):
        for kv in range(2):
            for d in offsets:
                @pl.when(exists(d))
                def _(d=d, kv=kv):
                    send_kv(h, d, kv).start()
            own_kv(h, kv).start()

    def own_w(h):
        return pltpu.make_async_copy(
            w_hbm.at[pl.ds(pl.multiple_of(h * HD, HD), HD), :],
            wbank.at[h, pl.ds(pl.multiple_of(group * HD, HD), HD), :],
            w_own.at[h],
        )

    def pair_w(h, owner):
        return pltpu.make_async_remote_copy(
            src_ref=w_hbm.at[pl.ds(pl.multiple_of(h * HD, HD), HD), :],
            dst_ref=wbank.at[h, pl.ds(pl.multiple_of(owner * HD, HD), HD), :],
            send_sem=pair_send.at[h],
            recv_sem=pair_recv.at[h],
            device_id={"head": sibling},
            device_id_type=MESH,
        )

    def part(owner, piece):
        return pl.ds(pl.multiple_of(owner * HD + piece * part_rows, part_rows), part_rows)

    def row_w(h, owner, other_row):
        return pltpu.make_async_remote_copy(
            src_ref=w_hbm.at[pl.ds(pl.multiple_of(h * HD + video * part_rows, part_rows), part_rows), :],
            dst_ref=wbank.at[h, part(owner, video), :],
            send_sem=row_send.at[h, other_row],
            recv_sem=row_recv.at[h, owner // 2],
            device_id={"head": other_row * 2 + core},
            device_id_type=MESH,
        )

    def spread_w(h, far_row, to_video):
        owner = far_row * 2 + core
        return pltpu.make_async_remote_copy(
            src_ref=wbank.at[h, part(owner, video), :],
            dst_ref=wbank.at[h, part(owner, video), :],
            send_sem=spread_send.at[h, far_row, to_video],
            recv_sem=spread_recv.at[h, far_row, video],
            device_id={"video": to_video},
            device_id_type=MESH,
        )

    def spread_in(h, far_row, from_video):
        owner = far_row * 2 + core
        return pltpu.make_async_remote_copy(
            src_ref=wbank.at[h, part(owner, from_video), :],
            dst_ref=wbank.at[h, part(owner, from_video), :],
            send_sem=spread_send.at[h, far_row, from_video],
            recv_sem=spread_recv.at[h, far_row, from_video],
            device_id={"video": from_video},
            device_id_type=MESH,
        )

    def last_w(h, far_row, piece, owner_core):
        owner = far_row * 2 + owner_core
        return pltpu.make_async_remote_copy(
            src_ref=wbank.at[h, part(owner, piece), :],
            dst_ref=wbank.at[h, part(owner, piece), :],
            send_sem=last_send.at[h, far_row, piece],
            recv_sem=last_recv.at[h, far_row, piece],
            device_id={"head": sibling},
            device_id_type=MESH,
        )

    far_rows = [(row + step) % rows_of_chips for step in range(1, rows_of_chips)]
    far_videos = [(video + step) % videos for step in range(1, videos)]

    def w_first(h):
        for far in far_rows:
            row_w(h, group, far).start()
        pair_w(h, group).start()
        own_w(h).start()

    def w_second(h):
        for far in far_rows:
            row_w(h, far * 2 + core, far).wait_recv()
            for other in far_videos:
                spread_w(h, far, other).start()
            last_w(h, far, video, core).start()

    def w_third(h):
        for far in far_rows:
            for other in far_videos:
                spread_in(h, far, other).wait_recv()
                last_w(h, far, other, core).start()

    def w_ready(h):
        own_w(h).wait()
        pair_w(h, sibling).wait_recv()
        for far in far_rows:
            for piece in range(videos):
                last_w(h, far, piece, 1 - core).wait_recv()

    def w_sent(h):
        pair_w(h, group).wait_send()
        for far in far_rows:
            row_w(h, group, far).wait_send()
            for other in far_videos:
                spread_w(h, far, other).wait_send()
            for piece in range(videos):
                last_w(h, far, piece, core).wait_send()

    def rows_ready(h):
        for g in range(groups):
            @pl.when(group != g)
            def _(g=g):
                recv_att(h, g).wait_recv()

            @pl.when(group == g)
            def _(g=g):
                own_att(h, g).wait()

    def project(h, last):
        w_ready(h)
        rows_ready(h)
        step = 512

        def block(b, carry):
            at = pl.ds(pl.multiple_of(b * step, step), step)
            term = jnp.dot(abank[h], wbank[h, :, at], preferred_element_type=jnp.float32)
            if last:
                out_ref[:, at] = (acc[:, at] + term).astype(out_ref.dtype)
            else:
                acc[:, at] += term
            return carry

        lax.fori_loop(0, width // step, block, 0)

    barrier = pltpu.get_barrier_semaphore()
    for other in far_videos:
        pl.semaphore_signal(barrier, inc=1, device_id={"video": other}, device_id_type=MESH)
    for d in offsets:
        @pl.when(exists(d))
        def _(d=d):
            pl.semaphore_signal(barrier, inc=1, device_id={"frame": slab + d}, device_id_type=MESH)
    for g in range(groups):
        @pl.when(group != g)
        def _(g=g):
            pl.semaphore_signal(barrier, inc=1, device_id={"head": g}, device_id_type=MESH)
    below = jnp.minimum(slab, reach)
    above = jnp.minimum(frames - 1 - slab, reach)
    pl.semaphore_wait(barrier, groups + videos - 2 + below + above)

    issue(0)
    if heads > 1:
        issue(1)
    for first in range(heads):
        w_first(first)
    acc[...] = jnp.zeros_like(acc)
    vcur[:, :, HD:] = jnp.ones((vcur.shape[0], TILE, HD), vcur.dtype)

    def one_head(h, carry):
        for kv in range(2):
            own_kv(h, kv).wait()
            for d in offsets:
                @pl.when(exists(d))
                def _(d=d, kv=kv):
                    recv_kv(h, d, kv).wait_recv()
        for kv in range(2):
            for d in offsets:
                @pl.when(exists(d))
                def _(d=d, kv=kv):
                    send_kv(h, d, kv).wait_send()

        @pl.when(h + 2 < heads)
        def _():
            issue(h + 2)

        for chunk in (2 * h, 2 * h + 1):
            @pl.when(chunk < heads)
            def _(chunk=chunk):
                w_second(chunk)
        for chunk in (2 * h - 2, 2 * h - 1):
            @pl.when((chunk >= 0) & (chunk < heads))
            def _(chunk=chunk):
                w_third(chunk)

        for d in [0] + offsets:
            @pl.when(exists(d))
            def _(d=d):
                for tile in range((reach + d) * tiles, (reach + d + 1) * tiles):
                    rows = slice(tile * TILE, (tile + 1) * TILE)
                    kcur[tile] = kbank[h, rows, :]
                    vcur[tile, :, :HD] = vbank[h, rows, :]

        scratch = (s0, s1)

        def score(t, j, tops):
            s_ref = scratch[t % 2]
            q_tile = q_ref[t * TILE:(t + 1) * TILE, lanes(h)]
            s = lax.dot_general(
                q_tile, kcur[ids_ref[t, j]],
                (((1,), (1,)), ((), ())), preferred_element_type=jnp.float32,
            )
            s_ref[:, j * TILE:(j + 1) * TILE] = s
            for c in range(TILE // HD):
                part = s[:, c * HD:(c + 1) * HD]
                tops = part if tops is None else jnp.maximum(tops, part)
            return tops

        tops = None
        for j in range(listed):
            tops = score(0, j, tops)
        for t in range(tiles):
            row_max = jnp.max(tops, axis=1, keepdims=True)
            tops = None
            total = None
            for j in range(0, listed, 2):
                if t + 1 < tiles:
                    tops = score(t + 1, j, tops)
                    tops = score(t + 1, j + 1, tops)
                s = scratch[t % 2][:, j * TILE:(j + 2) * TILE]
                weights = jnp.exp2((s - row_max) * EXP2_SCALE).astype(jnp.bfloat16)
                v_pair = jnp.concatenate([vcur[ids_ref[t, j]], vcur[ids_ref[t, j + 1]]], axis=0)
                term = jnp.dot(weights, v_pair, preferred_element_type=jnp.float32)
                total = term if total is None else total + term
            att[h, t * TILE:(t + 1) * TILE, :] = (total[:, :HD] / total[:, HD:]).astype(att.dtype)
            for owner in range(t * owners_per_tile, (t + 1) * owners_per_tile):
                @pl.when(group != owner)
                def _(owner=owner):
                    send_att(h, owner).start()

                @pl.when(group == owner)
                def _(owner=owner):
                    own_att(h, owner).start()

        @pl.when(h > 0)
        def _():
            project(h - 1, False)

        return carry

    lax.fori_loop(0, heads, one_head, 0)
    for chunk in range(max(0, 2 * (heads - 1)), heads):
        w_third(chunk)
    project(heads - 1, True)

    def finish(h, carry):
        for g in range(groups):
            @pl.when(group != g)
            def _(g=g):
                send_att(h, g).wait_send()
        w_sent(h)
        return carry

    lax.fori_loop(0, heads, finish, 0)


def on_device(query, keys, values, out_weight, tile_lists):
    frames = lax.axis_size("frame")
    groups = lax.axis_size("head")
    my_slab = lax.axis_index("frame")
    reach = min(2, (frames - 2) // 2)
    tokens, cols = query.shape
    heads = cols // HD
    tiles = tokens // TILE
    listed = tile_lists.shape[1]
    rows_out = tokens // groups
    bank_rows = (2 * reach + 1) * tokens
    ids = (tile_lists // tiles - my_slab + reach) * tiles + tile_lists % tiles
    videos = lax.axis_size("video")
    chip_rows = groups // 2
    width = out_weight.shape[1]
    return pl.pallas_call(
        functools.partial(attention_kernel, frames, groups, videos, reach),
        out_shape=jax.ShapeDtypeStruct((rows_out, width), jnp.bfloat16),
        in_specs=[
            pl.BlockSpec(memory_space=pltpu.SMEM),
            pl.BlockSpec(memory_space=pltpu.VMEM),
            pl.BlockSpec(memory_space=pl.ANY),
            pl.BlockSpec(memory_space=pl.ANY),
            pl.BlockSpec(memory_space=pl.ANY),
        ],
        out_specs=pl.BlockSpec(memory_space=pltpu.VMEM),
        scratch_shapes=[
            pltpu.VMEM((heads, bank_rows, HD), jnp.bfloat16),
            pltpu.VMEM((heads, bank_rows, HD), jnp.bfloat16),
            pltpu.VMEM((bank_rows // TILE, TILE, HD), jnp.bfloat16),
            pltpu.VMEM((bank_rows // TILE, TILE, 2 * HD), jnp.bfloat16),
            pltpu.VMEM((heads, tokens, HD), jnp.bfloat16),
            pltpu.VMEM((TILE, listed * TILE), jnp.float32),
            pltpu.VMEM((TILE, listed * TILE), jnp.float32),
            pltpu.VMEM((heads, rows_out, groups * HD), jnp.bfloat16),
            pltpu.VMEM((heads, groups * HD, width), jnp.bfloat16),
            pltpu.VMEM((rows_out, width), jnp.float32),
            pltpu.SemaphoreType.DMA((heads, 2 * reach + 1, 2)),
            pltpu.SemaphoreType.DMA((heads, 2 * reach + 1, 2)),
            pltpu.SemaphoreType.DMA((heads, 2)),
            pltpu.SemaphoreType.DMA((heads, groups)),
            pltpu.SemaphoreType.DMA((heads, groups)),
            pltpu.SemaphoreType.DMA((heads,)),
            pltpu.SemaphoreType.DMA((heads,)),
            pltpu.SemaphoreType.DMA((heads,)),
            pltpu.SemaphoreType.DMA((heads,)),
            pltpu.SemaphoreType.DMA((heads, chip_rows)),
            pltpu.SemaphoreType.DMA((heads, chip_rows)),
            pltpu.SemaphoreType.DMA((heads, chip_rows, videos)),
            pltpu.SemaphoreType.DMA((heads, chip_rows, videos)),
            pltpu.SemaphoreType.DMA((heads, chip_rows, videos)),
            pltpu.SemaphoreType.DMA((heads, chip_rows, videos)),
        ],
        compiler_params=pltpu.CompilerParams(
            collective_id=0, has_side_effects=True, vmem_limit_bytes=62 * 1024 * 1024
        ),
        cost_estimate=pl.CostEstimate(
            flops=4 * tokens * listed * TILE * cols,
            bytes_accessed=8 * tokens * cols,
            transcendentals=tokens * listed * TILE * heads,
        ),
    )(ids, query, keys, values, out_weight)


def solution(mesh):
    return jax.shard_map(
        on_device,
        mesh=mesh,
        in_specs=(
            P(("video", "frame"), "head"),
            P(("video", "frame"), "head"),
            P(("video", "frame"), "head"),
            P("head", None),
            P(("video", "frame"), None),
        ),
        out_specs=P(("video", "frame", "head"), None),
        check_vma=False,
    )
```

```python
import functools
import math

import jax
import jax.numpy as jnp
from jax import lax
from jax.experimental import pallas as pl
from jax.experimental.pallas import tpu as pltpu
from jax.sharding import PartitionSpec as P

HD = 128
TILE = 384
MESH = pl.DeviceIdType.MESH
EXP2_SCALE = math.log2(math.e) / math.sqrt(HD)


def attention_kernel(
    frames, groups, videos, reach, ids_ref, q_hbm, k_hbm, v_hbm, w_hbm, out_ref,
    q_ref, q_sem, kbank, vbank, kcur, vcur, att, s0, s1, abank, wbank, acc,
    kv_send, kv_recv, own_sem, a_send, a_recv, a_own,
    w_own, pair_send, pair_recv, row_send, row_recv, spread_send, spread_recv, last_send, last_recv,
):
    tokens, cols = q_hbm.shape
    heads = cols // HD
    tiles = tokens // TILE
    listed = ids_ref.shape[1]
    rows_out = tokens // groups
    owners_per_tile = TILE // rows_out
    slab = lax.axis_index("frame")
    group = lax.axis_index("head")
    video = lax.axis_index("video")
    core = group % 2
    row = group // 2
    rows_of_chips = groups // 2
    sibling = row * 2 + 1 - core
    part_rows = HD // videos
    width = acc.shape[1]
    offsets = [d for r in range(1, reach + 1) for d in (-r, r)]
    stores = ((k_hbm, kbank), (v_hbm, vbank))

    def exists(d):
        return (slab + d >= 0) & (slab + d < frames)

    def lanes(h):
        return pl.ds(pl.multiple_of(h * HD, HD), HD)

    def send_kv(h, d, kv):
        src, bank = stores[kv]
        return pltpu.make_async_remote_copy(
            src_ref=bank.at[h, pl.ds(reach * tokens, tokens), :],
            dst_ref=bank.at[h, pl.ds((reach - d) * tokens, tokens), :],
            send_sem=kv_send.at[h, reach + d, kv],
            recv_sem=kv_recv.at[h, reach - d, kv],
            device_id={"frame": slab + d},
            device_id_type=MESH,
        )

    def recv_kv(h, d, kv):
        src, bank = stores[kv]
        return pltpu.make_async_remote_copy(
            src_ref=bank.at[h, pl.ds(reach * tokens, tokens), :],
            dst_ref=bank.at[h, pl.ds((reach + d) * tokens, tokens), :],
            send_sem=kv_send.at[h, reach + d, kv],
            recv_sem=kv_recv.at[h, reach + d, kv],
            device_id={"frame": slab + d},
            device_id_type=MESH,
        )

    def own_kv(h, kv):
        src, bank = stores[kv]
        return pltpu.make_async_copy(
            src.at[:, lanes(h)],
            bank.at[h, pl.ds(reach * tokens, tokens), :],
            own_sem.at[h, kv],
        )

    def send_att(h, owner):
        return pltpu.make_async_remote_copy(
            src_ref=att.at[h, pl.ds(owner * rows_out, rows_out), :],
            dst_ref=abank.at[h, :, lanes(group)],
            send_sem=a_send.at[h, owner],
            recv_sem=a_recv.at[h, group],
            device_id={"head": owner},
            device_id_type=MESH,
        )

    def recv_att(h, sender):
        return pltpu.make_async_remote_copy(
            src_ref=att.at[h, pl.ds(0, rows_out), :],
            dst_ref=abank.at[h, :, lanes(sender)],
            send_sem=a_send.at[h, sender],
            recv_sem=a_recv.at[h, sender],
            device_id={"head": sender},
            device_id_type=MESH,
        )

    def own_att(h, owner):
        return pltpu.make_async_copy(
            att.at[h, pl.ds(owner * rows_out, rows_out), :],
            abank.at[h, :, lanes(owner)],
            a_own.at[h],
        )

    def issue(h):
        for kv in range(2):
            own_kv(h, kv).wait()
            for d in offsets:
                @pl.when(exists(d))
                def _(d=d, kv=kv):
                    send_kv(h, d, kv).start()

    def own_w(h):
        return pltpu.make_async_copy(
            w_hbm.at[pl.ds(pl.multiple_of(h * HD, HD), HD), :],
            wbank.at[h, pl.ds(pl.multiple_of(group * HD, HD), HD), :],
            w_own.at[h],
        )

    def pair_w(h, owner):
        return pltpu.make_async_remote_copy(
            src_ref=w_hbm.at[pl.ds(pl.multiple_of(h * HD, HD), HD), :],
            dst_ref=wbank.at[h, pl.ds(pl.multiple_of(owner * HD, HD), HD), :],
            send_sem=pair_send.at[h],
            recv_sem=pair_recv.at[h],
            device_id={"head": sibling},
            device_id_type=MESH,
        )

    def part(owner, piece):
        return pl.ds(pl.multiple_of(owner * HD + piece * part_rows, part_rows), part_rows)

    def row_w(h, owner, other_row):
        return pltpu.make_async_remote_copy(
            src_ref=w_hbm.at[pl.ds(pl.multiple_of(h * HD + video * part_rows, part_rows), part_rows), :],
            dst_ref=wbank.at[h, part(owner, video), :],
            send_sem=row_send.at[h, other_row],
            recv_sem=row_recv.at[h, owner // 2],
            device_id={"head": other_row * 2 + core},
            device_id_type=MESH,
        )

    def spread_w(h, far_row, to_video):
        owner = far_row * 2 + core
        return pltpu.make_async_remote_copy(
            src_ref=wbank.at[h, part(owner, video), :],
            dst_ref=wbank.at[h, part(owner, video), :],
            send_sem=spread_send.at[h, far_row, to_video],
            recv_sem=spread_recv.at[h, far_row, video],
            device_id={"video": to_video},
            device_id_type=MESH,
        )

    def spread_in(h, far_row, from_video):
        owner = far_row * 2 + core
        return pltpu.make_async_remote_copy(
            src_ref=wbank.at[h, part(owner, from_video), :],
            dst_ref=wbank.at[h, part(owner, from_video), :],
            send_sem=spread_send.at[h, far_row, from_video],
            recv_sem=spread_recv.at[h, far_row, from_video],
            device_id={"video": from_video},
            device_id_type=MESH,
        )

    def last_w(h, far_row, piece, owner_core):
        owner = far_row * 2 + owner_core
        return pltpu.make_async_remote_copy(
            src_ref=wbank.at[h, part(owner, piece), :],
            dst_ref=wbank.at[h, part(owner, piece), :],
            send_sem=last_send.at[h, far_row, piece],
            recv_sem=last_recv.at[h, far_row, piece],
            device_id={"head": sibling},
            device_id_type=MESH,
        )

    far_rows = [(row + step) % rows_of_chips for step in range(1, rows_of_chips)]
    far_videos = [(video + step) % videos for step in range(1, videos)]

    def w_first(h):
        for far in far_rows:
            row_w(h, group, far).start()
        pair_w(h, group).start()
        own_w(h).start()

    def w_second(h):
        for far in far_rows:
            row_w(h, far * 2 + core, far).wait_recv()
            for other in far_videos:
                spread_w(h, far, other).start()
            last_w(h, far, video, core).start()

    def w_third(h):
        for far in far_rows:
            for other in far_videos:
                spread_in(h, far, other).wait_recv()
                last_w(h, far, other, core).start()

    def w_ready(h):
        own_w(h).wait()
        pair_w(h, sibling).wait_recv()
        for far in far_rows:
            for piece in range(videos):
                last_w(h, far, piece, 1 - core).wait_recv()

    def w_sent(h):
        pair_w(h, group).wait_send()
        for far in far_rows:
            row_w(h, group, far).wait_send()
            for other in far_videos:
                spread_w(h, far, other).wait_send()
            for piece in range(videos):
                last_w(h, far, piece, core).wait_send()

    def rows_ready(h):
        for g in range(groups):
            @pl.when(group != g)
            def _(g=g):
                recv_att(h, g).wait_recv()

            @pl.when(group == g)
            def _(g=g):
                own_att(h, g).wait()

    def project(h, last):
        w_ready(h)
        rows_ready(h)
        step = 512

        def block(b, carry):
            at = pl.ds(pl.multiple_of(b * step, step), step)
            term = jnp.dot(abank[h], wbank[h, :, at], preferred_element_type=jnp.float32)
            if last:
                out_ref[:, at] = (acc[:, at] + term).astype(out_ref.dtype)
            else:
                acc[:, at] += term
            return carry

        lax.fori_loop(0, width // step, block, 0)

    for early in range(heads):
        for kv in range(2):
            own_kv(early, kv).start()

    barrier = pltpu.get_barrier_semaphore()
    for other in far_videos:
        pl.semaphore_signal(barrier, inc=1, device_id={"video": other}, device_id_type=MESH)
    for d in offsets:
        @pl.when(exists(d))
        def _(d=d):
            pl.semaphore_signal(barrier, inc=1, device_id={"frame": slab + d}, device_id_type=MESH)
    for g in range(groups):
        @pl.when(group != g)
        def _(g=g):
            pl.semaphore_signal(barrier, inc=1, device_id={"head": g}, device_id_type=MESH)
    below = jnp.minimum(slab, reach)
    above = jnp.minimum(frames - 1 - slab, reach)
    pl.semaphore_wait(barrier, groups + videos - 2 + below + above)

    issue(0)
    if heads > 1:
        issue(1)
    q_load = pltpu.make_async_copy(q_hbm, q_ref, q_sem)
    q_load.start()
    for first in range(heads):
        w_first(first)
    acc[...] = jnp.zeros_like(acc)
    vcur[:, :, HD:] = jnp.ones((vcur.shape[0], TILE, HD), vcur.dtype)

    q_load.wait()
    first_id = (reach - slab) * tiles

    def listed_tile(t, j):
        return jnp.clip(ids_ref[t, j] + first_id, 0, kcur.shape[0] - 1)

    def one_head(h, carry):
        for d in offsets:
            @pl.when(exists(d))
            def _(d=d):
                recv_kv(h, d, 0).wait_recv()
        for d in [0] + offsets:
            @pl.when(exists(d))
            def _(d=d):
                for tile in range((reach + d) * tiles, (reach + d + 1) * tiles):
                    kcur[tile] = kbank[h, tile * TILE:(tile + 1) * TILE, :]

        scratch = (s0, s1)

        def score(t, j, tops):
            s_ref = scratch[t % 2]
            q_tile = q_ref[t * TILE:(t + 1) * TILE, lanes(h)]
            s = lax.dot_general(
                q_tile, kcur[listed_tile(t, j)],
                (((1,), (1,)), ((), ())), preferred_element_type=jnp.float32,
            )
            s_ref[:, j * TILE:(j + 1) * TILE] = s
            for c in range(TILE // HD):
                part = s[:, c * HD:(c + 1) * HD]
                tops = part if tops is None else jnp.maximum(tops, part)
            return tops

        tops = None
        for j in range(listed):
            tops = score(0, j, tops)

        for d in offsets:
            @pl.when(exists(d))
            def _(d=d):
                recv_kv(h, d, 1).wait_recv()
        for kv in range(2):
            for d in offsets:
                @pl.when(exists(d))
                def _(d=d, kv=kv):
                    send_kv(h, d, kv).wait_send()

        @pl.when(h + 2 < heads)
        def _():
            issue(h + 2)

        for chunk in (2 * h, 2 * h + 1):
            @pl.when(chunk < heads)
            def _(chunk=chunk):
                w_second(chunk)
        for chunk in (2 * h - 2, 2 * h - 1):
            @pl.when((chunk >= 0) & (chunk < heads))
            def _(chunk=chunk):
                w_third(chunk)

        for d in [0] + offsets:
            @pl.when(exists(d))
            def _(d=d):
                for tile in range((reach + d) * tiles, (reach + d + 1) * tiles):
                    vcur[tile, :, :HD] = vbank[h, tile * TILE:(tile + 1) * TILE, :]

        for t in range(tiles):
            row_max = jnp.max(tops, axis=1, keepdims=True)
            tops = None
            total = None
            for j in range(0, listed, 2):
                if t + 1 < tiles:
                    tops = score(t + 1, j, tops)
                    tops = score(t + 1, j + 1, tops)
                s = scratch[t % 2][:, j * TILE:(j + 2) * TILE]
                weights = jnp.exp2((s - row_max) * EXP2_SCALE).astype(jnp.bfloat16)
                v_pair = jnp.concatenate([vcur[listed_tile(t, j)], vcur[listed_tile(t, j + 1)]], axis=0)
                term = jnp.dot(weights, v_pair, preferred_element_type=jnp.float32)
                total = term if total is None else total + term
            att[h, t * TILE:(t + 1) * TILE, :] = (total[:, :HD] / total[:, HD:]).astype(att.dtype)
            for owner in range(t * owners_per_tile, (t + 1) * owners_per_tile):
                @pl.when(group != owner)
                def _(owner=owner):
                    send_att(h, owner).start()

                @pl.when(group == owner)
                def _(owner=owner):
                    own_att(h, owner).start()

        @pl.when(h > 0)
        def _():
            project(h - 1, False)

        return carry

    lax.fori_loop(0, heads, one_head, 0)
    for chunk in range(max(0, 2 * (heads - 1)), heads):
        w_third(chunk)
    project(heads - 1, True)

    def finish(h, carry):
        for g in range(groups):
            @pl.when(group != g)
            def _(g=g):
                send_att(h, g).wait_send()
        w_sent(h)
        return carry

    lax.fori_loop(0, heads, finish, 0)


def on_device(query, keys, values, out_weight, tile_lists):
    frames = lax.axis_size("frame")
    groups = lax.axis_size("head")
    reach = min(2, (frames - 2) // 2)
    tokens, cols = query.shape
    heads = cols // HD
    listed = tile_lists.shape[1]
    rows_out = tokens // groups
    bank_rows = (2 * reach + 1) * tokens
    videos = lax.axis_size("video")
    chip_rows = groups // 2
    width = out_weight.shape[1]
    return pl.pallas_call(
        functools.partial(attention_kernel, frames, groups, videos, reach),
        out_shape=jax.ShapeDtypeStruct((rows_out, width), jnp.bfloat16),
        in_specs=[
            pl.BlockSpec(memory_space=pltpu.SMEM),
            pl.BlockSpec(memory_space=pl.ANY),
            pl.BlockSpec(memory_space=pl.ANY),
            pl.BlockSpec(memory_space=pl.ANY),
            pl.BlockSpec(memory_space=pl.ANY),
        ],
        out_specs=pl.BlockSpec(memory_space=pltpu.VMEM),
        scratch_shapes=[
            pltpu.VMEM((tokens, cols), jnp.bfloat16),
            pltpu.SemaphoreType.DMA,
            pltpu.VMEM((heads, bank_rows, HD), jnp.bfloat16),
            pltpu.VMEM((heads, bank_rows, HD), jnp.bfloat16),
            pltpu.VMEM((bank_rows // TILE, TILE, HD), jnp.bfloat16),
            pltpu.VMEM((bank_rows // TILE, TILE, 2 * HD), jnp.bfloat16),
            pltpu.VMEM((heads, tokens, HD), jnp.bfloat16),
            pltpu.VMEM((TILE, listed * TILE), jnp.float32),
            pltpu.VMEM((TILE, listed * TILE), jnp.float32),
            pltpu.VMEM((heads, rows_out, groups * HD), jnp.bfloat16),
            pltpu.VMEM((heads, groups * HD, width), jnp.bfloat16),
            pltpu.VMEM((rows_out, width), jnp.float32),
            pltpu.SemaphoreType.DMA((heads, 2 * reach + 1, 2)),
            pltpu.SemaphoreType.DMA((heads, 2 * reach + 1, 2)),
            pltpu.SemaphoreType.DMA((heads, 2)),
            pltpu.SemaphoreType.DMA((heads, groups)),
            pltpu.SemaphoreType.DMA((heads, groups)),
            pltpu.SemaphoreType.DMA((heads,)),
            pltpu.SemaphoreType.DMA((heads,)),
            pltpu.SemaphoreType.DMA((heads,)),
            pltpu.SemaphoreType.DMA((heads,)),
            pltpu.SemaphoreType.DMA((heads, chip_rows)),
            pltpu.SemaphoreType.DMA((heads, chip_rows)),
            pltpu.SemaphoreType.DMA((heads, chip_rows, videos)),
            pltpu.SemaphoreType.DMA((heads, chip_rows, videos)),
            pltpu.SemaphoreType.DMA((heads, chip_rows, videos)),
            pltpu.SemaphoreType.DMA((heads, chip_rows, videos)),
        ],
        compiler_params=pltpu.CompilerParams(
            collective_id=0, has_side_effects=True, vmem_limit_bytes=62 * 1024 * 1024
        ),
        cost_estimate=pl.CostEstimate(
            flops=4 * tokens * listed * TILE * cols,
            bytes_accessed=8 * tokens * cols,
            transcendentals=tokens * listed * TILE * heads,
        ),
    )(tile_lists, query, keys, values, out_weight)


def solution(mesh):
    return jax.shard_map(
        on_device,
        mesh=mesh,
        in_specs=(
            P(("video", "frame"), "head"),
            P(("video", "frame"), "head"),
            P(("video", "frame"), "head"),
            P("head", None),
            P(("video", "frame"), None),
        ),
        out_specs=P(("video", "frame", "head"), None),
        check_vma=False,
    )
```

```python
import functools
import math

import jax
import jax.numpy as jnp
from jax import lax
from jax.experimental import pallas as pl
from jax.experimental.pallas import tpu as pltpu
from jax.sharding import PartitionSpec as P

HD = 128
TILE = 384
MESH = pl.DeviceIdType.MESH
EXP2_SCALE = math.log2(math.e) / math.sqrt(HD)


def attention_kernel(
    frames, groups, videos, reach, ids_ref, q_hbm, k_hbm, v_hbm, w_hbm, out_ref,
    q_ref, q_sem, kbank, vbank, kcur, vcur, att, pbank, tops, abank, wbank, acc,
    kv_send, kv_recv, own_sem, a_send, a_recv, a_own,
    w_own, pair_send, pair_recv, row_send, row_recv, spread_send, spread_recv, last_send, last_recv,
):
    tokens, cols = q_hbm.shape
    heads = cols // HD
    tiles = tokens // TILE
    listed = ids_ref.shape[1]
    rows_out = tokens // groups
    owners_per_tile = TILE // rows_out
    slab = lax.axis_index("frame")
    group = lax.axis_index("head")
    video = lax.axis_index("video")
    core = group % 2
    row = group // 2
    rows_of_chips = groups // 2
    sibling = row * 2 + 1 - core
    part_rows = HD // videos
    width = acc.shape[1]
    offsets = [d for r in range(1, reach + 1) for d in (-r, r)]
    stores = ((k_hbm, kbank), (v_hbm, vbank))

    def exists(d):
        return (slab + d >= 0) & (slab + d < frames)

    def lanes(h):
        return pl.ds(pl.multiple_of(h * HD, HD), HD)

    def send_kv(h, d, kv):
        src, bank = stores[kv]
        return pltpu.make_async_remote_copy(
            src_ref=bank.at[h, pl.ds(reach * tokens, tokens), :],
            dst_ref=bank.at[h, pl.ds((reach - d) * tokens, tokens), :],
            send_sem=kv_send.at[h, reach + d, kv],
            recv_sem=kv_recv.at[h, reach - d, kv],
            device_id={"frame": slab + d},
            device_id_type=MESH,
        )

    def recv_kv(h, d, kv):
        src, bank = stores[kv]
        return pltpu.make_async_remote_copy(
            src_ref=bank.at[h, pl.ds(reach * tokens, tokens), :],
            dst_ref=bank.at[h, pl.ds((reach + d) * tokens, tokens), :],
            send_sem=kv_send.at[h, reach + d, kv],
            recv_sem=kv_recv.at[h, reach + d, kv],
            device_id={"frame": slab + d},
            device_id_type=MESH,
        )

    def own_kv(h, kv):
        src, bank = stores[kv]
        return pltpu.make_async_copy(
            src.at[:, lanes(h)],
            bank.at[h, pl.ds(reach * tokens, tokens), :],
            own_sem.at[h, kv],
        )

    def send_att(h, owner):
        return pltpu.make_async_remote_copy(
            src_ref=att.at[h, pl.ds(owner * rows_out, rows_out), :],
            dst_ref=abank.at[h, :, lanes(group)],
            send_sem=a_send.at[h, owner],
            recv_sem=a_recv.at[h, group],
            device_id={"head": owner},
            device_id_type=MESH,
        )

    def recv_att(h, sender):
        return pltpu.make_async_remote_copy(
            src_ref=att.at[h, pl.ds(0, rows_out), :],
            dst_ref=abank.at[h, :, lanes(sender)],
            send_sem=a_send.at[h, sender],
            recv_sem=a_recv.at[h, sender],
            device_id={"head": sender},
            device_id_type=MESH,
        )

    def own_att(h, owner):
        return pltpu.make_async_copy(
            att.at[h, pl.ds(owner * rows_out, rows_out), :],
            abank.at[h, :, lanes(owner)],
            a_own.at[h],
        )

    def issue(h, kv):
        own_kv(h, kv).wait()
        for d in offsets:
            @pl.when(exists(d))
            def _(d=d):
                send_kv(h, d, kv).start()

    def own_w(h):
        return pltpu.make_async_copy(
            w_hbm.at[pl.ds(pl.multiple_of(h * HD, HD), HD), :],
            wbank.at[h, pl.ds(pl.multiple_of(group * HD, HD), HD), :],
            w_own.at[h],
        )

    def pair_w(h, owner):
        return pltpu.make_async_remote_copy(
            src_ref=w_hbm.at[pl.ds(pl.multiple_of(h * HD, HD), HD), :],
            dst_ref=wbank.at[h, pl.ds(pl.multiple_of(owner * HD, HD), HD), :],
            send_sem=pair_send.at[h],
            recv_sem=pair_recv.at[h],
            device_id={"head": sibling},
            device_id_type=MESH,
        )

    def part(owner, piece):
        return pl.ds(pl.multiple_of(owner * HD + piece * part_rows, part_rows), part_rows)

    def row_w(h, owner, other_row):
        return pltpu.make_async_remote_copy(
            src_ref=w_hbm.at[pl.ds(pl.multiple_of(h * HD + video * part_rows, part_rows), part_rows), :],
            dst_ref=wbank.at[h, part(owner, video), :],
            send_sem=row_send.at[h, other_row],
            recv_sem=row_recv.at[h, owner // 2],
            device_id={"head": other_row * 2 + core},
            device_id_type=MESH,
        )

    def spread_w(h, far_row, to_video):
        owner = far_row * 2 + core
        return pltpu.make_async_remote_copy(
            src_ref=wbank.at[h, part(owner, video), :],
            dst_ref=wbank.at[h, part(owner, video), :],
            send_sem=spread_send.at[h, far_row, to_video],
            recv_sem=spread_recv.at[h, far_row, video],
            device_id={"video": to_video},
            device_id_type=MESH,
        )

    def spread_in(h, far_row, from_video):
        owner = far_row * 2 + core
        return pltpu.make_async_remote_copy(
            src_ref=wbank.at[h, part(owner, from_video), :],
            dst_ref=wbank.at[h, part(owner, from_video), :],
            send_sem=spread_send.at[h, far_row, from_video],
            recv_sem=spread_recv.at[h, far_row, from_video],
            device_id={"video": from_video},
            device_id_type=MESH,
        )

    def last_w(h, far_row, piece, owner_core):
        owner = far_row * 2 + owner_core
        return pltpu.make_async_remote_copy(
            src_ref=wbank.at[h, part(owner, piece), :],
            dst_ref=wbank.at[h, part(owner, piece), :],
            send_sem=last_send.at[h, far_row, piece],
            recv_sem=last_recv.at[h, far_row, piece],
            device_id={"head": sibling},
            device_id_type=MESH,
        )

    far_rows = [(row + step) % rows_of_chips for step in range(1, rows_of_chips)]
    far_videos = [(video + step) % videos for step in range(1, videos)]

    def w_first(h):
        for far in far_rows:
            row_w(h, group, far).start()
        pair_w(h, group).start()
        own_w(h).start()

    def w_second(h):
        for far in far_rows:
            row_w(h, far * 2 + core, far).wait_recv()
            for other in far_videos:
                spread_w(h, far, other).start()
            last_w(h, far, video, core).start()

    def w_third(h):
        for far in far_rows:
            for other in far_videos:
                spread_in(h, far, other).wait_recv()
                last_w(h, far, other, core).start()

    def w_ready(h):
        own_w(h).wait()
        pair_w(h, sibling).wait_recv()
        for far in far_rows:
            for piece in range(videos):
                last_w(h, far, piece, 1 - core).wait_recv()

    def w_sent(h):
        pair_w(h, group).wait_send()
        for far in far_rows:
            row_w(h, group, far).wait_send()
            for other in far_videos:
                spread_w(h, far, other).wait_send()
            for piece in range(videos):
                last_w(h, far, piece, core).wait_send()

    def rows_ready(h):
        for g in range(groups):
            @pl.when(group != g)
            def _(g=g):
                recv_att(h, g).wait_recv()

            @pl.when(group == g)
            def _(g=g):
                own_att(h, g).wait()

    def project(h, last):
        w_ready(h)
        rows_ready(h)
        step = 512

        def block(b, carry):
            at = pl.ds(pl.multiple_of(b * step, step), step)
            term = jnp.dot(abank[h], wbank[h, :, at], preferred_element_type=jnp.float32)
            if last:
                out_ref[:, at] = (acc[:, at] + term).astype(out_ref.dtype)
            else:
                acc[:, at] += term
            return carry

        lax.fori_loop(0, width // step, block, 0)

    for early in range(heads):
        for kv in range(2):
            own_kv(early, kv).start()

    barrier = pltpu.get_barrier_semaphore()
    for other in far_videos:
        pl.semaphore_signal(barrier, inc=1, device_id={"video": other}, device_id_type=MESH)
    for d in offsets:
        @pl.when(exists(d))
        def _(d=d):
            pl.semaphore_signal(barrier, inc=1, device_id={"frame": slab + d}, device_id_type=MESH)
    for g in range(groups):
        @pl.when(group != g)
        def _(g=g):
            pl.semaphore_signal(barrier, inc=1, device_id={"head": g}, device_id_type=MESH)
    below = jnp.minimum(slab, reach)
    above = jnp.minimum(frames - 1 - slab, reach)
    pl.semaphore_wait(barrier, groups + videos - 2 + below + above)

    issue(0, 0)
    issue(0, 1)
    q_load = pltpu.make_async_copy(q_hbm, q_ref, q_sem)
    q_load.start()
    for first in range(heads):
        w_first(first)
    acc[...] = jnp.zeros_like(acc)
    vcur[:, :, HD:] = jnp.ones((vcur.shape[0], TILE, HD), vcur.dtype)

    q_load.wait()
    first_id = (reach - slab) * tiles

    def listed_tile(t, j):
        return jnp.clip(ids_ref[t, j] + first_id, 0, kcur.shape[0] - 1)

    def one_head(h, carry):
        for d in offsets:
            @pl.when(exists(d))
            def _(d=d):
                recv_kv(h, d, 0).wait_recv()
        for d in [0] + offsets:
            @pl.when(exists(d))
            def _(d=d):
                for tile in range((reach + d) * tiles, (reach + d + 1) * tiles):
                    kcur[tile] = kbank[h, tile * TILE:(tile + 1) * TILE, :]

        @pl.when(h + 1 < heads)
        def _():
            issue(h + 1, 0)

        for t in range(tiles):
            q_tile = q_ref[t * TILE:(t + 1) * TILE, lanes(h)]
            for i in range(listed // 2):
                k_pair = jnp.concatenate([kcur[listed_tile(t, 2 * i)], kcur[listed_tile(t, 2 * i + 1)]], axis=0)
                s = lax.dot_general(
                    q_tile, k_pair, (((1,), (1,)), ((), ())), preferred_element_type=jnp.float32
                )
                top = jnp.max(s, axis=1, keepdims=True)
                weights = jnp.exp2((s - top) * EXP2_SCALE).astype(jnp.bfloat16)
                pbank[t, :, 2 * i * TILE:2 * (i + 1) * TILE] = weights
                tops[t, i] = jnp.broadcast_to(top, (TILE, HD))

        for d in offsets:
            @pl.when(exists(d))
            def _(d=d):
                recv_kv(h, d, 1).wait_recv()

        @pl.when(h + 1 < heads)
        def _():
            issue(h + 1, 1)

        for chunk in (2 * h, 2 * h + 1):
            @pl.when(chunk < heads)
            def _(chunk=chunk):
                w_second(chunk)
        for chunk in (2 * h - 2, 2 * h - 1):
            @pl.when((chunk >= 0) & (chunk < heads))
            def _(chunk=chunk):
                w_third(chunk)

        for d in [0] + offsets:
            @pl.when(exists(d))
            def _(d=d):
                for tile in range((reach + d) * tiles, (reach + d + 1) * tiles):
                    vcur[tile, :, :HD] = vbank[h, tile * TILE:(tile + 1) * TILE, :]

        for t in range(tiles):
            pairs = range(listed // 2)
            row_max = functools.reduce(jnp.maximum, [tops[t, i] for i in pairs])
            mixed = 0.0
            row_total = 0.0
            for i in pairs:
                v_pair = jnp.concatenate([vcur[listed_tile(t, 2 * i)], vcur[listed_tile(t, 2 * i + 1)]], axis=0)
                term = jnp.dot(
                    pbank[t, :, 2 * i * TILE:2 * (i + 1) * TILE], v_pair, preferred_element_type=jnp.float32
                )
                share = jnp.exp2((tops[t, i] - row_max) * EXP2_SCALE)
                mixed = mixed + term[:, :HD] * share
                row_total = row_total + term[:, HD:] * share
            att[h, t * TILE:(t + 1) * TILE, :] = (mixed / row_total).astype(att.dtype)
            for owner in range(t * owners_per_tile, (t + 1) * owners_per_tile):
                @pl.when(group != owner)
                def _(owner=owner):
                    send_att(h, owner).start()

                @pl.when(group == owner)
                def _(owner=owner):
                    own_att(h, owner).start()

        @pl.when(h > 0)
        def _():
            project(h - 1, False)

        return carry

    lax.fori_loop(0, heads, one_head, 0)
    for chunk in range(max(0, 2 * (heads - 1)), heads):
        w_third(chunk)
    project(heads - 1, True)

    def finish(h, carry):
        for g in range(groups):
            @pl.when(group != g)
            def _(g=g):
                send_att(h, g).wait_send()
        for kv in range(2):
            for d in offsets:
                @pl.when(exists(d))
                def _(d=d, kv=kv):
                    send_kv(h, d, kv).wait_send()
        w_sent(h)
        return carry

    lax.fori_loop(0, heads, finish, 0)


def on_device(query, keys, values, out_weight, tile_lists):
    frames = lax.axis_size("frame")
    groups = lax.axis_size("head")
    reach = min(2, (frames - 2) // 2)
    tokens, cols = query.shape
    heads = cols // HD
    listed = tile_lists.shape[1]
    rows_out = tokens // groups
    bank_rows = (2 * reach + 1) * tokens
    videos = lax.axis_size("video")
    chip_rows = groups // 2
    width = out_weight.shape[1]
    return pl.pallas_call(
        functools.partial(attention_kernel, frames, groups, videos, reach),
        out_shape=jax.ShapeDtypeStruct((rows_out, width), jnp.bfloat16),
        in_specs=[
            pl.BlockSpec(memory_space=pltpu.SMEM),
            pl.BlockSpec(memory_space=pl.ANY),
            pl.BlockSpec(memory_space=pl.ANY),
            pl.BlockSpec(memory_space=pl.ANY),
            pl.BlockSpec(memory_space=pl.ANY),
        ],
        out_specs=pl.BlockSpec(memory_space=pltpu.VMEM),
        scratch_shapes=[
            pltpu.VMEM((tokens, cols), jnp.bfloat16),
            pltpu.SemaphoreType.DMA,
            pltpu.VMEM((heads, bank_rows, HD), jnp.bfloat16),
            pltpu.VMEM((heads, bank_rows, HD), jnp.bfloat16),
            pltpu.VMEM((bank_rows // TILE, TILE, HD), jnp.bfloat16),
            pltpu.VMEM((bank_rows // TILE, TILE, 2 * HD), jnp.bfloat16),
            pltpu.VMEM((heads, tokens, HD), jnp.bfloat16),
            pltpu.VMEM((tokens // TILE, TILE, listed * TILE), jnp.bfloat16),
            pltpu.VMEM((tokens // TILE, listed // 2, TILE, HD), jnp.float32),
            pltpu.VMEM((heads, rows_out, groups * HD), jnp.bfloat16),
            pltpu.VMEM((heads, groups * HD, width), jnp.bfloat16),
            pltpu.VMEM((rows_out, width), jnp.float32),
            pltpu.SemaphoreType.DMA((heads, 2 * reach + 1, 2)),
            pltpu.SemaphoreType.DMA((heads, 2 * reach + 1, 2)),
            pltpu.SemaphoreType.DMA((heads, 2)),
            pltpu.SemaphoreType.DMA((heads, groups)),
            pltpu.SemaphoreType.DMA((heads, groups)),
            pltpu.SemaphoreType.DMA((heads,)),
            pltpu.SemaphoreType.DMA((heads,)),
            pltpu.SemaphoreType.DMA((heads,)),
            pltpu.SemaphoreType.DMA((heads,)),
            pltpu.SemaphoreType.DMA((heads, chip_rows)),
            pltpu.SemaphoreType.DMA((heads, chip_rows)),
            pltpu.SemaphoreType.DMA((heads, chip_rows, videos)),
            pltpu.SemaphoreType.DMA((heads, chip_rows, videos)),
            pltpu.SemaphoreType.DMA((heads, chip_rows, videos)),
            pltpu.SemaphoreType.DMA((heads, chip_rows, videos)),
        ],
        compiler_params=pltpu.CompilerParams(
            collective_id=0, has_side_effects=True, vmem_limit_bytes=62 * 1024 * 1024
        ),
        cost_estimate=pl.CostEstimate(
            flops=4 * tokens * listed * TILE * cols,
            bytes_accessed=8 * tokens * cols,
            transcendentals=tokens * listed * TILE * heads,
        ),
    )(tile_lists, query, keys, values, out_weight)


def solution(mesh):
    return jax.shard_map(
        on_device,
        mesh=mesh,
        in_specs=(
            P(("video", "frame"), "head"),
            P(("video", "frame"), "head"),
            P(("video", "frame"), "head"),
            P("head", None),
            P(("video", "frame"), None),
        ),
        out_specs=P(("video", "frame", "head"), None),
        check_vma=False,
    )
```

```python
import functools
import math

import jax
import jax.numpy as jnp
from jax import lax
from jax.experimental import pallas as pl
from jax.experimental.pallas import tpu as pltpu
from jax.sharding import PartitionSpec as P

HD = 128
TILE = 384
MESH = pl.DeviceIdType.MESH
EXP2_SCALE = math.log2(math.e) / math.sqrt(HD)


def attention_kernel(
    frames, groups, videos, reach, ids_ref, q_hbm, k_hbm, v_hbm, w_hbm, out_ref,
    q_ref, q_sem, kbank, vbank, kcur, vcur, att, s0, s1, abank, wbank, acc,
    kv_send, kv_recv, own_sem, a_send, a_recv, a_own,
    w_own, pair_send, pair_recv, row_send, row_recv, spread_send, spread_recv, last_send, last_recv,
):
    tokens, cols = q_hbm.shape
    heads = cols // HD
    tiles = tokens // TILE
    listed = ids_ref.shape[1]
    rows_out = tokens // groups
    owners_per_tile = TILE // rows_out
    slab = lax.axis_index("frame")
    group = lax.axis_index("head")
    video = lax.axis_index("video")
    core = group % 2
    row = group // 2
    rows_of_chips = groups // 2
    sibling = row * 2 + 1 - core
    part_rows = HD // videos
    width = acc.shape[1]
    offsets = [d for r in range(1, reach + 1) for d in (-r, r)]
    stores = ((k_hbm, kbank), (v_hbm, vbank))

    def exists(d):
        return (slab + d >= 0) & (slab + d < frames)

    def lanes(h):
        return pl.ds(pl.multiple_of(h * HD, HD), HD)

    def send_kv(h, d, kv):
        src, bank = stores[kv]
        return pltpu.make_async_remote_copy(
            src_ref=bank.at[h, pl.ds(reach * tokens, tokens), :],
            dst_ref=bank.at[h, pl.ds((reach - d) * tokens, tokens), :],
            send_sem=kv_send.at[h, reach + d, kv],
            recv_sem=kv_recv.at[h, reach - d, kv],
            device_id={"frame": slab + d},
            device_id_type=MESH,
        )

    def recv_kv(h, d, kv):
        src, bank = stores[kv]
        return pltpu.make_async_remote_copy(
            src_ref=bank.at[h, pl.ds(reach * tokens, tokens), :],
            dst_ref=bank.at[h, pl.ds((reach + d) * tokens, tokens), :],
            send_sem=kv_send.at[h, reach + d, kv],
            recv_sem=kv_recv.at[h, reach + d, kv],
            device_id={"frame": slab + d},
            device_id_type=MESH,
        )

    def own_kv(h, kv):
        src, bank = stores[kv]
        return pltpu.make_async_copy(
            src.at[:, lanes(h)],
            bank.at[h, pl.ds(reach * tokens, tokens), :],
            own_sem.at[h, kv],
        )

    def send_att(h, owner):
        return pltpu.make_async_remote_copy(
            src_ref=att.at[h, pl.ds(owner * rows_out, rows_out), :],
            dst_ref=abank.at[h, :, lanes(group)],
            send_sem=a_send.at[h, owner],
            recv_sem=a_recv.at[h, group],
            device_id={"head": owner},
            device_id_type=MESH,
        )

    def recv_att(h, sender):
        return pltpu.make_async_remote_copy(
            src_ref=att.at[h, pl.ds(0, rows_out), :],
            dst_ref=abank.at[h, :, lanes(sender)],
            send_sem=a_send.at[h, sender],
            recv_sem=a_recv.at[h, sender],
            device_id={"head": sender},
            device_id_type=MESH,
        )

    def own_att(h, owner):
        return pltpu.make_async_copy(
            att.at[h, pl.ds(owner * rows_out, rows_out), :],
            abank.at[h, :, lanes(owner)],
            a_own.at[h],
        )

    def sent(h, kv):
        for d in offsets:
            @pl.when(exists(d))
            def _(d=d):
                send_kv(h, d, kv).wait_send()

    def issue(h, after=None):
        for kv in range(2):
            own_kv(h, kv).wait()
            if after is not None:
                sent(after, kv)
            for d in offsets:
                @pl.when(exists(d))
                def _(d=d, kv=kv):
                    send_kv(h, d, kv).start()

    def own_w(h):
        return pltpu.make_async_copy(
            w_hbm.at[pl.ds(pl.multiple_of(h * HD, HD), HD), :],
            wbank.at[h, pl.ds(pl.multiple_of(group * HD, HD), HD), :],
            w_own.at[h],
        )

    def pair_w(h, owner):
        return pltpu.make_async_remote_copy(
            src_ref=w_hbm.at[pl.ds(pl.multiple_of(h * HD, HD), HD), :],
            dst_ref=wbank.at[h, pl.ds(pl.multiple_of(owner * HD, HD), HD), :],
            send_sem=pair_send.at[h],
            recv_sem=pair_recv.at[h],
            device_id={"head": sibling},
            device_id_type=MESH,
        )

    def part(owner, piece):
        return pl.ds(pl.multiple_of(owner * HD + piece * part_rows, part_rows), part_rows)

    def row_w(h, owner, other_row):
        return pltpu.make_async_remote_copy(
            src_ref=w_hbm.at[pl.ds(pl.multiple_of(h * HD + video * part_rows, part_rows), part_rows), :],
            dst_ref=wbank.at[h, part(owner, video), :],
            send_sem=row_send.at[h, other_row],
            recv_sem=row_recv.at[h, owner // 2],
            device_id={"head": other_row * 2 + core},
            device_id_type=MESH,
        )

    def spread_w(h, far_row, to_video):
        owner = far_row * 2 + core
        return pltpu.make_async_remote_copy(
            src_ref=wbank.at[h, part(owner, video), :],
            dst_ref=wbank.at[h, part(owner, video), :],
            send_sem=spread_send.at[h, far_row, to_video],
            recv_sem=spread_recv.at[h, far_row, video],
            device_id={"video": to_video},
            device_id_type=MESH,
        )

    def spread_in(h, far_row, from_video):
        owner = far_row * 2 + core
        return pltpu.make_async_remote_copy(
            src_ref=wbank.at[h, part(owner, from_video), :],
            dst_ref=wbank.at[h, part(owner, from_video), :],
            send_sem=spread_send.at[h, far_row, from_video],
            recv_sem=spread_recv.at[h, far_row, from_video],
            device_id={"video": from_video},
            device_id_type=MESH,
        )

    def last_w(h, far_row, piece, owner_core):
        owner = far_row * 2 + owner_core
        return pltpu.make_async_remote_copy(
            src_ref=wbank.at[h, part(owner, piece), :],
            dst_ref=wbank.at[h, part(owner, piece), :],
            send_sem=last_send.at[h, far_row, piece],
            recv_sem=last_recv.at[h, far_row, piece],
            device_id={"head": sibling},
            device_id_type=MESH,
        )

    far_rows = [(row + step) % rows_of_chips for step in range(1, rows_of_chips)]
    far_videos = [(video + step) % videos for step in range(1, videos)]

    def w_first(h):
        for far in far_rows:
            row_w(h, group, far).start()
        pair_w(h, group).start()
        own_w(h).start()

    def w_second(h):
        for far in far_rows:
            row_w(h, far * 2 + core, far).wait_recv()
            for other in far_videos:
                spread_w(h, far, other).start()
            last_w(h, far, video, core).start()

    def w_third(h):
        for far in far_rows:
            for other in far_videos:
                spread_in(h, far, other).wait_recv()
                last_w(h, far, other, core).start()

    def w_ready(h):
        own_w(h).wait()
        pair_w(h, sibling).wait_recv()
        for far in far_rows:
            for piece in range(videos):
                last_w(h, far, piece, 1 - core).wait_recv()

    def w_sent(h):
        pair_w(h, group).wait_send()
        for far in far_rows:
            row_w(h, group, far).wait_send()
            for other in far_videos:
                spread_w(h, far, other).wait_send()
            for piece in range(videos):
                last_w(h, far, piece, core).wait_send()

    def rows_ready(h):
        for g in range(groups):
            @pl.when(group != g)
            def _(g=g):
                recv_att(h, g).wait_recv()

            @pl.when(group == g)
            def _(g=g):
                own_att(h, g).wait()

    def project(h, last):
        w_ready(h)
        rows_ready(h)
        step = 512

        def block(b, carry):
            at = pl.ds(pl.multiple_of(b * step, step), step)
            term = jnp.dot(abank[h], wbank[h, :, at], preferred_element_type=jnp.float32)
            if last:
                out_ref[:, at] = (acc[:, at] + term).astype(out_ref.dtype)
            else:
                acc[:, at] += term
            return carry

        lax.fori_loop(0, width // step, block, 0)

    for early in range(heads):
        for kv in range(2):
            own_kv(early, kv).start()

    barrier = pltpu.get_barrier_semaphore()
    for other in far_videos:
        pl.semaphore_signal(barrier, inc=1, device_id={"video": other}, device_id_type=MESH)
    for d in offsets:
        @pl.when(exists(d))
        def _(d=d):
            pl.semaphore_signal(barrier, inc=1, device_id={"frame": slab + d}, device_id_type=MESH)
    for g in range(groups):
        @pl.when(group != g)
        def _(g=g):
            pl.semaphore_signal(barrier, inc=1, device_id={"head": g}, device_id_type=MESH)
    below = jnp.minimum(slab, reach)
    above = jnp.minimum(frames - 1 - slab, reach)
    pl.semaphore_wait(barrier, groups + videos - 2 + below + above)

    issue(0)
    q_load = pltpu.make_async_copy(q_hbm, q_ref, q_sem)
    q_load.start()
    for first in range(heads):
        w_first(first)
    acc[...] = jnp.zeros_like(acc)
    vcur[:, :, HD:] = jnp.ones((vcur.shape[0], TILE, HD), vcur.dtype)

    q_load.wait()
    if heads > 1:
        issue(1, after=0)
    else:
        sent(0, 0)
        sent(0, 1)
    first_id = (reach - slab) * tiles

    def listed_tile(t, j):
        return jnp.clip(ids_ref[t, j] + first_id, 0, kcur.shape[0] - 1)

    def one_head(h, carry):
        for d in offsets:
            @pl.when(exists(d))
            def _(d=d):
                recv_kv(h, d, 0).wait_recv()
        for d in [0] + offsets:
            @pl.when(exists(d))
            def _(d=d):
                for tile in range((reach + d) * tiles, (reach + d + 1) * tiles):
                    kcur[tile] = kbank[h, tile * TILE:(tile + 1) * TILE, :]

        scratch = (s0, s1)

        def score(t, j, tops):
            s_ref = scratch[t % 2]
            q_tile = q_ref[t * TILE:(t + 1) * TILE, lanes(h)]
            s = lax.dot_general(
                q_tile, kcur[listed_tile(t, j)],
                (((1,), (1,)), ((), ())), preferred_element_type=jnp.float32,
            )
            s_ref[:, j * TILE:(j + 1) * TILE] = s
            for c in range(TILE // HD):
                part = s[:, c * HD:(c + 1) * HD]
                tops = part if tops is None else jnp.maximum(tops, part)
            return tops

        tops = None
        for j in range(listed):
            tops = score(0, j, tops)

        for d in offsets:
            @pl.when(exists(d))
            def _(d=d):
                recv_kv(h, d, 1).wait_recv()
        @pl.when(h > 0)
        def _():
            sent(h, 0)
            sent(h, 1)

        @pl.when(h + 2 < heads)
        def _():
            issue(h + 2)

        for chunk in (2 * h, 2 * h + 1):
            @pl.when(chunk < heads)
            def _(chunk=chunk):
                w_second(chunk)
        for chunk in (2 * h - 2, 2 * h - 1):
            @pl.when((chunk >= 0) & (chunk < heads))
            def _(chunk=chunk):
                w_third(chunk)

        for d in [0] + offsets:
            @pl.when(exists(d))
            def _(d=d):
                for tile in range((reach + d) * tiles, (reach + d + 1) * tiles):
                    vcur[tile, :, :HD] = vbank[h, tile * TILE:(tile + 1) * TILE, :]

        for t in range(tiles):
            row_max = jnp.max(tops, axis=1, keepdims=True)
            tops = None
            total = None
            for j in range(0, listed, 2):
                if t + 1 < tiles:
                    tops = score(t + 1, j, tops)
                    tops = score(t + 1, j + 1, tops)
                s = scratch[t % 2][:, j * TILE:(j + 2) * TILE]
                weights = jnp.exp2((s - row_max) * EXP2_SCALE).astype(jnp.bfloat16)
                v_pair = jnp.concatenate([vcur[listed_tile(t, j)], vcur[listed_tile(t, j + 1)]], axis=0)
                term = jnp.dot(weights, v_pair, preferred_element_type=jnp.float32)
                total = term if total is None else total + term
            att[h, t * TILE:(t + 1) * TILE, :] = (total[:, :HD] / total[:, HD:]).astype(att.dtype)
            for owner in range(t * owners_per_tile, (t + 1) * owners_per_tile):
                @pl.when(group != owner)
                def _(owner=owner):
                    send_att(h, owner).start()

                @pl.when(group == owner)
                def _(owner=owner):
                    own_att(h, owner).start()

        @pl.when(h > 0)
        def _():
            project(h - 1, False)

        return carry

    lax.fori_loop(0, heads, one_head, 0)
    for chunk in range(max(0, 2 * (heads - 1)), heads):
        w_third(chunk)
    project(heads - 1, True)

    def finish(h, carry):
        for g in range(groups):
            @pl.when(group != g)
            def _(g=g):
                send_att(h, g).wait_send()
        w_sent(h)
        return carry

    lax.fori_loop(0, heads, finish, 0)


def on_device(query, keys, values, out_weight, tile_lists):
    frames = lax.axis_size("frame")
    groups = lax.axis_size("head")
    reach = min(2, (frames - 2) // 2)
    tokens, cols = query.shape
    heads = cols // HD
    listed = tile_lists.shape[1]
    rows_out = tokens // groups
    bank_rows = (2 * reach + 1) * tokens
    videos = lax.axis_size("video")
    chip_rows = groups // 2
    width = out_weight.shape[1]
    return pl.pallas_call(
        functools.partial(attention_kernel, frames, groups, videos, reach),
        out_shape=jax.ShapeDtypeStruct((rows_out, width), jnp.bfloat16),
        in_specs=[
            pl.BlockSpec(memory_space=pltpu.SMEM),
            pl.BlockSpec(memory_space=pl.ANY),
            pl.BlockSpec(memory_space=pl.ANY),
            pl.BlockSpec(memory_space=pl.ANY),
            pl.BlockSpec(memory_space=pl.ANY),
        ],
        out_specs=pl.BlockSpec(memory_space=pltpu.VMEM),
        scratch_shapes=[
            pltpu.VMEM((tokens, cols), jnp.bfloat16),
            pltpu.SemaphoreType.DMA,
            pltpu.VMEM((heads, bank_rows, HD), jnp.bfloat16),
            pltpu.VMEM((heads, bank_rows, HD), jnp.bfloat16),
            pltpu.VMEM((bank_rows // TILE, TILE, HD), jnp.bfloat16),
            pltpu.VMEM((bank_rows // TILE, TILE, 2 * HD), jnp.bfloat16),
            pltpu.VMEM((heads, tokens, HD), jnp.bfloat16),
            pltpu.VMEM((TILE, listed * TILE), jnp.float32),
            pltpu.VMEM((TILE, listed * TILE), jnp.float32),
            pltpu.VMEM((heads, rows_out, groups * HD), jnp.bfloat16),
            pltpu.VMEM((heads, groups * HD, width), jnp.bfloat16),
            pltpu.VMEM((rows_out, width), jnp.float32),
            pltpu.SemaphoreType.DMA((heads, 2 * reach + 1, 2)),
            pltpu.SemaphoreType.DMA((heads, 2 * reach + 1, 2)),
            pltpu.SemaphoreType.DMA((heads, 2)),
            pltpu.SemaphoreType.DMA((heads, groups)),
            pltpu.SemaphoreType.DMA((heads, groups)),
            pltpu.SemaphoreType.DMA((heads,)),
            pltpu.SemaphoreType.DMA((heads,)),
            pltpu.SemaphoreType.DMA((heads,)),
            pltpu.SemaphoreType.DMA((heads,)),
            pltpu.SemaphoreType.DMA((heads, chip_rows)),
            pltpu.SemaphoreType.DMA((heads, chip_rows)),
            pltpu.SemaphoreType.DMA((heads, chip_rows, videos)),
            pltpu.SemaphoreType.DMA((heads, chip_rows, videos)),
            pltpu.SemaphoreType.DMA((heads, chip_rows, videos)),
            pltpu.SemaphoreType.DMA((heads, chip_rows, videos)),
        ],
        compiler_params=pltpu.CompilerParams(
            collective_id=0, has_side_effects=True, vmem_limit_bytes=62 * 1024 * 1024
        ),
        cost_estimate=pl.CostEstimate(
            flops=4 * tokens * listed * TILE * cols,
            bytes_accessed=8 * tokens * cols,
            transcendentals=tokens * listed * TILE * heads,
        ),
    )(tile_lists, query, keys, values, out_weight)


def solution(mesh):
    return jax.shard_map(
        on_device,
        mesh=mesh,
        in_specs=(
            P(("video", "frame"), "head"),
            P(("video", "frame"), "head"),
            P(("video", "frame"), "head"),
            P("head", None),
            P(("video", "frame"), None),
        ),
        out_specs=P(("video", "frame", "head"), None),
        check_vma=False,
    )
```
